128 devices in a mesh: seq: 32 (over z, x, core), head: 4 (over y).
Axes of the slice: x: 4, y: 4, z: 4, core: 2. Of those that a mesh axis runs over, the one named last changes fastest.
Arguments:
- query_in: bfloat16 [32768, 2048], P(('seq', 'head')), may hold values from -12 to 12
- key_in: bfloat16 [32768, 2048], P(('seq', 'head')), may hold values from -12 to 12
- value_in: bfloat16 [32768, 2048], P(('seq', 'head')), may hold values from -6 to 6
- out_grad: bfloat16 [32768, 2048], P(('seq', 'head')), may hold values from -6 to 6
- pattern: int32 [256, 256], replicated, may hold values from 0 to 1, as said below
Outputs:
- attended: bfloat16 [32768, 2048], P(('seq', 'head'))
- query_grad: bfloat16 [32768, 2048], P(('seq', 'head'))
- key_grad: bfloat16 [32768, 2048], P(('seq', 'head'))
- value_grad: bfloat16 [32768, 2048], P(('seq', 'head'))
The draws below stay inside these ranges and needn't reach their ends.
Inputs may be any that keep to these rules, and one draw needn't show every extreme that they name: `pattern`: Symmetric. Row 0, column 0 and every entry with |a - b| <= 1 are 1. Every other 1 at (a, b) joins blocks of two different groups of 8 consecutive blocks, and two groups share at most one such pair.
All inputs are finite; a program needn't handle non-finite values.
Results may differ from the reference program's by a relative error of at most 0.0075.
The reference program's roundings to bfloat16 on the way (of `weights` and `grad_scores`) count: a program that leaves them out, or rounds other values in their place, can miss the bound.
Values may be sent and summed in bfloat16 or wider, within the bound.
A program may use at most 256 MiB of HBM per device.

```python
import jax
import jax.numpy as jnp
from jax import lax

HEADS = 16
HEAD_DIM = 128
BLOCK = 128
WIDTH = 2048
FRAMES = 32768
BLOCKS = 256
BLOCKS_DEV = 8
LINKS = 35


def plant_points(key):
    subkeys = jax.random.split(key, 5)
    query_row = jax.random.randint(subkeys[0], (BLOCKS,), 0, BLOCK)
    first_key = jax.random.randint(subkeys[1], (BLOCKS,), 0, BLOCK)
    second_key = (first_key + jax.random.randint(subkeys[2], (BLOCKS,), 1, BLOCK)) % BLOCK
    strength = jax.random.uniform(subkeys[3], (BLOCKS,), minval=4.0, maxval=12.0)
    signs = jnp.where(jax.random.uniform(subkeys[4], (WIDTH,)) < 0.5, -1.0, 1.0)
    return (query_row, first_key, second_key, strength, signs)


def normal_base(key):
    return jnp.clip(jax.random.normal(key, (FRAMES, WIDTH)), -6.0, 6.0)


def draw_query_in(key, part):
    planted = plant_points(key)
    key = jax.random.fold_in(key, 3)
    base = normal_base(key)
    base = base.reshape(BLOCKS, BLOCK, WIDTH)
    positions = jnp.arange(BLOCK)
    chosen = positions[None, :] == planted[0][:, None]
    vector = planted[3][:, None, None] * planted[4][None, None, :]
    return jnp.where(chosen[:, :, None], vector, base).reshape(FRAMES, WIDTH).astype(jnp.bfloat16)


def draw_key_in(key, part):
    planted = plant_points(key)
    key = jax.random.fold_in(key, 5)
    base = normal_base(key)
    base = base.reshape(BLOCKS, BLOCK, WIDTH)
    positions = jnp.arange(BLOCK)
    first_hit = positions[None, :] == planted[1][:, None]
    second_hit = positions[None, :] == planted[2][:, None]
    vector = planted[3][:, None, None] * planted[4][None, None, :]
    field = jnp.where(first_hit[:, :, None], vector, base)
    return jnp.where(second_hit[:, :, None], 0.99 * vector, field).reshape(FRAMES, WIDTH).astype(jnp.bfloat16)


def draw_pattern(key, part):
    key = jax.random.fold_in(key, 7)
    subkeys = jax.random.split(key, 3)
    groups = BLOCKS // BLOCKS_DEV
    row_pick = jax.random.randint(subkeys[0], (groups, groups), 0, BLOCKS_DEV)
    col_pick = jax.random.randint(subkeys[1], (groups, groups), 0, BLOCKS_DEV)
    present = jax.random.randint(subkeys[2], (groups, groups), 0, 4) > 0
    row_group = jnp.arange(groups, dtype=jnp.int32)[:, None]
    col_group = jnp.arange(groups, dtype=jnp.int32)[None, :]
    chosen = (present & (row_group < col_group)).astype(jnp.int32)
    blocks = jnp.arange(BLOCKS, dtype=jnp.int32)
    row_hot = (blocks[None, None, :] == (row_group * BLOCKS_DEV + row_pick)[:, :, None]).astype(jnp.int32) * chosen[:, :, None]
    col_hot = (blocks[None, None, :] == (col_group * BLOCKS_DEV + col_pick)[:, :, None]).astype(jnp.int32)
    link_count = jnp.einsum('pqr,pqc->rc', row_hot, col_hot)
    near_band = (jnp.abs(blocks[:, None] - blocks[None, :]) <= 1).astype(jnp.int32)
    global_edge = ((blocks[:, None] == 0) | (blocks[None, :] == 0)).astype(jnp.int32)
    return jnp.minimum(link_count + link_count.T + near_band + global_edge, 1).astype(jnp.int32)


def level_of(own_key, shape, shards, smallest, largest):
    level, own = 1.0, jax.random.fold_in(own_key, 6)
    for position, blocks in shards:
        draws = jnp.exp(jax.random.uniform(jax.random.fold_in(own, position), (blocks,), jnp.float32, smallest / len(shards), largest / len(shards)))
        level = level * jnp.repeat(draws, shape[position] // blocks).reshape([-1 if axis == position else 1 for axis in range(len(shape))])
    return level


def scatter_about(stream_key, shape, scale, bound, shards=(), held_as=jnp.bfloat16):
    array = scale * jax.random.normal(stream_key, shape, jnp.float32)
    if shards:
        array = array * level_of(stream_key, shape, shards, -0.22, 0.18)
    return jnp.clip(array, -bound, bound).astype(held_as)


def setup_inputs(seed: int = 0) -> dict:
    keys = jax.random.split(jax.random.key(seed), 6)
    return {
        "query_in": draw_query_in(jax.random.fold_in(keys[5], 71), 0),
        "key_in": draw_key_in(jax.random.fold_in(keys[5], 71), 0),
        "value_in": scatter_about(keys[2], (FRAMES, WIDTH), 1.0, 6.0, ((0, 128),)),
        "out_grad": scatter_about(keys[3], (FRAMES, WIDTH), 1.0, 6.0, ((0, 128),)),
        "pattern": draw_pattern(jax.random.fold_in(keys[5], 71), 0),
    }


big_negative = -1.0e30


def key_list(pattern_row):
    block_total = pattern_row.shape[0]
    ranking = pattern_row * (2 * block_total) + (block_total - 1 - jnp.arange(block_total, dtype=jnp.int32))
    unused, key_index = lax.top_k(ranking, LINKS)
    key_index = key_index.astype(jnp.int32)
    return key_index, jnp.take(pattern_row, key_index).astype(jnp.float32)


def masked_scores(queries, keys_blk, live_keys):
    scores = jnp.einsum('qhe,dkhe->hqdk', queries.astype(jnp.float32), keys_blk.astype(jnp.float32)) * (HEAD_DIM ** -0.5)
    return jnp.where(live_keys[None, None, :, None] > 0, scores, big_negative)


def forward_tile(queries, keys_blk, values_blk, live_keys):
    scores = masked_scores(queries, keys_blk, live_keys)
    row_top = jnp.max(scores, axis=(2, 3))
    exp_total = jnp.sum(jnp.exp(scores - row_top[:, :, None, None]), axis=(2, 3))
    row_lse = row_top + jnp.log(exp_total)
    weights = jnp.exp(scores - row_lse[:, :, None, None]).astype(jnp.bfloat16)
    tile_out = jnp.einsum('hqdk,dkhe->qhe', weights.astype(jnp.float32), values_blk.astype(jnp.float32))
    return row_lse, tile_out.astype(jnp.bfloat16)


def query_tile(queries, grads, row_lse, row_delta, keys_blk, values_blk, live_keys):
    scores = masked_scores(queries, keys_blk, live_keys)
    weights = jnp.exp(scores - row_lse[:, :, None, None]).astype(jnp.bfloat16)
    grad_weights = jnp.einsum('qhe,dkhe->hqdk', grads.astype(jnp.float32), values_blk.astype(jnp.float32))
    grad_scores = (weights.astype(jnp.float32) * (grad_weights - row_delta[:, :, None, None])).astype(jnp.bfloat16)
    result = jnp.einsum('hqdk,dkhe->qhe', grad_scores.astype(jnp.float32), keys_blk.astype(jnp.float32)) * (HEAD_DIM ** -0.5)
    return result.astype(jnp.bfloat16)


def key_tile(key_one, value_one, queries, grads, row_lse, row_delta, live_rows):
    scores = jnp.einsum('dqhe,khe->hdqk', queries.astype(jnp.float32), key_one.astype(jnp.float32)) * (HEAD_DIM ** -0.5)
    scores = jnp.where(live_rows[None, :, None, None] > 0, scores, big_negative)
    weights = jnp.exp(scores - jnp.transpose(row_lse, (1, 0, 2))[:, :, :, None]).astype(jnp.bfloat16)
    grad_weights = jnp.einsum('dqhe,khe->hdqk', grads.astype(jnp.float32), value_one.astype(jnp.float32))
    grad_scores = (weights.astype(jnp.float32) * (grad_weights - jnp.transpose(row_delta, (1, 0, 2))[:, :, :, None])).astype(jnp.bfloat16)
    key_part = jnp.einsum('hdqk,dqhe->khe', grad_scores.astype(jnp.float32), queries.astype(jnp.float32)) * (HEAD_DIM ** -0.5)
    value_part = jnp.einsum('hdqk,dqhe->khe', weights.astype(jnp.float32), grads.astype(jnp.float32))
    return key_part.astype(jnp.bfloat16), value_part.astype(jnp.bfloat16)


def reference(query_in, key_in, value_in, out_grad, pattern):
    block_shape = (BLOCKS, BLOCK, HEADS, HEAD_DIM)
    queries = query_in.reshape(block_shape)
    key_blocks = key_in.reshape(block_shape)
    value_blocks = value_in.reshape(block_shape)
    grad_blocks = out_grad.reshape(block_shape)
    rows_all = jnp.arange(BLOCKS, dtype=jnp.int32)

    def forward_row(row_id):
        key_index, live_keys = key_list(pattern[row_id])
        return forward_tile(queries[row_id], key_blocks[key_index], value_blocks[key_index], live_keys)

    row_lse, outputs = lax.map(forward_row, rows_all)
    first_lse, first_out = forward_tile(queries[0], key_blocks, value_blocks, pattern[0].astype(jnp.float32))
    row_lse = row_lse.at[0].set(first_lse)
    outputs = outputs.at[0].set(first_out)
    row_delta = jnp.transpose(jnp.sum(grad_blocks.astype(jnp.float32) * outputs.astype(jnp.float32), axis=3), (0, 2, 1))

    def query_row(row_id):
        key_index, live_keys = key_list(pattern[row_id])
        return query_tile(queries[row_id], grad_blocks[row_id], row_lse[row_id], row_delta[row_id], key_blocks[key_index], value_blocks[key_index], live_keys)

    query_grads = lax.map(query_row, rows_all)
    query_grads = query_grads.at[0].set(query_tile(queries[0], grad_blocks[0], row_lse[0], row_delta[0], key_blocks, value_blocks, pattern[0].astype(jnp.float32)))

    def key_row(col_id):
        row_index, live_rows = key_list(pattern[col_id])
        return key_tile(key_blocks[col_id], value_blocks[col_id], queries[row_index], grad_blocks[row_index], row_lse[row_index], row_delta[row_index], live_rows)

    key_grads, value_grads = lax.map(key_row, rows_all)
    first_key, first_value = key_tile(key_blocks[0], value_blocks[0], queries, grad_blocks, row_lse, row_delta, pattern[:, 0].astype(jnp.float32))
    key_grads = key_grads.at[0].set(first_key)
    value_grads = value_grads.at[0].set(first_value)
    flat = (FRAMES, WIDTH)
    return outputs.reshape(flat), query_grads.reshape(flat), key_grads.reshape(flat), value_grads.reshape(flat)
```

```python
import functools

import jax
import jax.numpy as jnp
from jax import lax
from jax.experimental import pallas as pl
from jax.experimental.pallas import tpu as pltpu
from jax.sharding import PartitionSpec as P

HEAD_DIM = 128
BLOCK = 128
SCALE = HEAD_DIM ** (-0.5)
NEG = -1e30
MESH = pl.DeviceIdType.MESH
ANY = pl.BlockSpec(memory_space=pl.ANY)
SMEM = pl.BlockSpec(memory_space=pltpu.SMEM)
F32, BF16 = jnp.float32, jnp.bfloat16


def nt(a, b):
    return lax.dot_general(a, b, (((1,), (1,)), ((), ())), preferred_element_type=F32)


def tn(a, b):
    return lax.dot_general(a, b, (((0,), (0,)), ((), ())), preferred_element_type=F32)


def nn(a, b):
    return jnp.dot(a, b, preferred_element_type=F32)


def barrier_with(axis, me, count):
    sem = pltpu.get_barrier_semaphore()

    def greet(step, carry):
        pl.semaphore_signal(
            sem, inc=1, device_id={axis: lax.rem(me + step, count)}, device_id_type=MESH
        )
        return carry

    lax.fori_loop(1, count, greet, 0)
    pl.semaphore_wait(sem, count - 1)


def heads_in_kernel(count, narr, *refs):
    xs, outs = refs[:narr], refs[narr : 2 * narr]
    send, recv, local = refs[2 * narr :]
    me = lax.axis_index("head")
    width = xs[0].shape[1] // count
    barrier_with("head", me, count)
    copies = []
    for a in range(narr):
        for step in range(1, count):
            peer = lax.rem(me + step, count)
            copies.append(
                pltpu.make_async_remote_copy(
                    src_ref=xs[a].at[:, pl.ds(pl.multiple_of(peer * width, width), width)],
                    dst_ref=outs[a].at[me],
                    send_sem=send.at[a, step],
                    recv_sem=recv.at[a, step],
                    device_id={"head": peer},
                    device_id_type=MESH,
                )
            )
            copies[-1].start()
        copies.append(
            pltpu.make_async_copy(
                xs[a].at[:, pl.ds(pl.multiple_of(me * width, width), width)],
                outs[a].at[me],
                local.at[a],
            )
        )
        copies[-1].start()
    for copy in copies:
        copy.wait()


def heads_in(xs, ident):
    count, narr = lax.axis_size("head"), len(xs)
    rows, width = xs[0].shape
    outs = pl.pallas_call(
        functools.partial(heads_in_kernel, count, narr),
        out_shape=[jax.ShapeDtypeStruct((count, rows, width // count), x.dtype) for x in xs],
        in_specs=[ANY] * narr,
        out_specs=[ANY] * narr,
        scratch_shapes=[
            pltpu.SemaphoreType.DMA((narr, count)),
            pltpu.SemaphoreType.DMA((narr, count)),
            pltpu.SemaphoreType.DMA((narr,)),
        ],
        compiler_params=pltpu.CompilerParams(collective_id=ident, has_side_effects=True),
        name="heads_in",
    )(*xs)
    return [o.reshape(count * rows, width // count) for o in outs]


def heads_out_kernel(count, narr, *refs):
    xs, outs = refs[:narr], refs[narr : 2 * narr]
    send, recv, local = refs[2 * narr :]
    me = lax.axis_index("head")
    width = xs[0].shape[1]
    rows = xs[0].shape[0] // count
    barrier_with("head", me, count)
    mine = pl.ds(pl.multiple_of(me * width, width), width)
    copies = []
    for a in range(narr):
        for step in range(1, count):
            peer = lax.rem(me + step, count)
            copies.append(
                pltpu.make_async_remote_copy(
                    src_ref=xs[a].at[pl.ds(pl.multiple_of(peer * rows, rows), rows)],
                    dst_ref=outs[a].at[:, mine],
                    send_sem=send.at[a, step],
                    recv_sem=recv.at[a, step],
                    device_id={"head": peer},
                    device_id_type=MESH,
                )
            )
            copies[-1].start()
        copies.append(
            pltpu.make_async_copy(
                xs[a].at[pl.ds(pl.multiple_of(me * rows, rows), rows)],
                outs[a].at[:, mine],
                local.at[a],
            )
        )
        copies[-1].start()
    for copy in copies:
        copy.wait()


def heads_out(xs, ident):
    count, narr = lax.axis_size("head"), len(xs)
    frames, width = xs[0].shape
    return pl.pallas_call(
        functools.partial(heads_out_kernel, count, narr),
        out_shape=[jax.ShapeDtypeStruct((frames // count, width * count), x.dtype) for x in xs],
        in_specs=[ANY] * narr,
        out_specs=[ANY] * narr,
        scratch_shapes=[
            pltpu.SemaphoreType.DMA((narr, count)),
            pltpu.SemaphoreType.DMA((narr, count)),
            pltpu.SemaphoreType.DMA((narr,)),
        ],
        compiler_params=pltpu.CompilerParams(collective_id=ident, has_side_effects=True),
        name="heads_out",
    )(*xs)


def edges_kernel(count, q, k, v, g, edge, first, send, recv, scatter_send, scatter_recv, local, near):
    me = lax.axis_index("seq")
    arrays = (q, k, v, g)
    frames = q.shape[0]
    barrier_with("seq", me, count)
    right, left = lax.rem(me + 1, count), lax.rem(me + count - 1, count)
    copies = []
    for a, x in enumerate((k, v)):
        for side, (peer, rows) in enumerate(
            ((right, pl.ds(frames - BLOCK, BLOCK)), (left, pl.ds(0, BLOCK)))
        ):
            copies.append(
                pltpu.make_async_remote_copy(
                    src_ref=x.at[rows],
                    dst_ref=edge.at[a, side],
                    send_sem=near.at[0, a, side],
                    recv_sem=near.at[1, a, side],
                    device_id={"seq": peer},
                    device_id_type=MESH,
                )
            )
            copies[-1].start()

    def piece(a, unit):
        rows = pl.multiple_of(lax.rem(unit, 8) * 16, 16)
        columns = pl.multiple_of((unit // 8) * HEAD_DIM, HEAD_DIM)
        return arrays[a].at[pl.ds(rows, 16), pl.ds(columns, HEAD_DIM)]

    def scatter_copy(a, unit):
        return pltpu.make_async_remote_copy(
            src_ref=piece(a, unit),
            dst_ref=first.at[a, unit],
            send_sem=scatter_send.at[a, unit],
            recv_sem=scatter_recv.at[a],
            device_id={"seq": unit},
            device_id_type=MESH,
        )

    @pl.when(me == 0)
    def _():
        def start(unit, carry):
            for a in range(4):
                scatter_copy(a, unit).start()
            return carry

        lax.fori_loop(1, count, start, 0)
        for a in range(4):
            own = pltpu.make_async_copy(piece(a, 0), first.at[a, 0], local.at[a])
            own.start()
        for a in range(4):
            pltpu.make_async_copy(piece(a, 0), first.at[a, 0], local.at[a]).wait()

    @pl.when(me > 0)
    def _():
        for a in range(4):
            pltpu.make_async_copy(first.at[a, me], first.at[a, me], scatter_recv.at[a]).wait()

    def pass_copy(step, slot):
        peer = lax.rem(me + step, count)
        return pltpu.make_async_remote_copy(
            src_ref=first.at[:, me],
            dst_ref=first.at[:, me],
            send_sem=send.at[step],
            recv_sem=recv.at[step],
            device_id={"seq": peer},
            device_id_type=MESH,
        )

    def start_pass(step, carry):
        pass_copy(step, me).start()
        return carry

    def wait_pass(step, carry):
        source = lax.rem(me + count - step, count)
        landed = first.at[:, source]
        pltpu.make_async_copy(landed, landed, recv.at[step]).wait()
        mine = first.at[:, me]
        pltpu.make_async_copy(mine, mine, send.at[step]).wait()
        return carry

    lax.fori_loop(1, count, start_pass, 0)
    lax.fori_loop(1, count, wait_pass, 0)

    @pl.when(me == 0)
    def _():
        def done(unit, carry):
            for a in range(4):
                pltpu.make_async_copy(piece(a, unit), piece(a, unit), scatter_send.at[a, unit]).wait()
            return carry

        lax.fori_loop(1, count, done, 0)

    for copy in copies:
        copy.wait()


def edges(q, k, v, g, ident):
    count = lax.axis_size("seq")
    width = q.shape[1]
    return pl.pallas_call(
        functools.partial(edges_kernel, count),
        out_shape=[
            jax.ShapeDtypeStruct((2, 2, BLOCK, width), BF16),
            jax.ShapeDtypeStruct((4, count, 16, HEAD_DIM), BF16),
        ],
        in_specs=[ANY] * 4,
        out_specs=[ANY] * 2,
        scratch_shapes=[
            pltpu.SemaphoreType.DMA((count,)),
            pltpu.SemaphoreType.DMA((count,)),
            pltpu.SemaphoreType.DMA((4, count)),
            pltpu.SemaphoreType.DMA((4,)),
            pltpu.SemaphoreType.DMA((4,)),
            pltpu.SemaphoreType.DMA((2, 2, 2)),
        ],
        compiler_params=pltpu.CompilerParams(collective_id=ident, has_side_effects=True),
        name="edges",
    )(q, k, v, g)


def exchange_kernel(count, nall, nsame, nside, *refs):
    ins = refs[: nall + nsame + nside]
    outs = refs[nall + nsame + nside : 2 * (nall + nsame + nside)]
    send, recv, local, near = refs[2 * (nall + nsame + nside) :]
    me = lax.axis_index("seq")
    barrier_with("seq", me, count)
    right, left = lax.rem(me + 1, count), lax.rem(me + count - 1, count)
    far = nall + nsame

    def source(a, peer):
        return ins[a].at[peer] if a < nall else ins[a]

    def copy(a, step):
        peer = lax.rem(me + step, count)
        return pltpu.make_async_remote_copy(
            src_ref=source(a, peer),
            dst_ref=outs[a].at[me],
            send_sem=send.at[a, step],
            recv_sem=recv.at[a, step],
            device_id={"seq": peer},
            device_id_type=MESH,
        )

    def start(step, carry):
        for a in range(far):
            copy(a, step).start()
        return carry

    lax.fori_loop(1, count, start, 0)
    copies = []
    for a in range(far):
        copies.append(pltpu.make_async_copy(source(a, me), outs[a].at[me], local.at[a]))
        copies[-1].start()
    for a in range(nside):
        for side, peer in enumerate((right, left)):
            copies.append(
                pltpu.make_async_remote_copy(
                    src_ref=ins[far + a].at[side],
                    dst_ref=outs[far + a].at[side],
                    send_sem=near.at[0, a, side],
                    recv_sem=near.at[1, a, side],
                    device_id={"seq": peer},
                    device_id_type=MESH,
                )
            )
            copies[-1].start()

    def finish(step, carry):
        for a in range(far):
            landed = outs[a].at[lax.rem(me + count - step, count)]
            pltpu.make_async_copy(landed, landed, recv.at[a, step]).wait()
            sent = source(a, lax.rem(me + step, count))
            pltpu.make_async_copy(sent, sent, send.at[a, step]).wait()
        return carry

    lax.fori_loop(1, count, finish, 0)
    for c in copies:
        c.wait()


def exchange(ident, to_each=(), to_all=(), to_sides=()):
    count = lax.axis_size("seq")
    ins = list(to_each) + list(to_all) + list(to_sides)
    shapes = [x.shape for x in to_each]
    shapes += [(count,) + x.shape for x in to_all]
    shapes += [x.shape for x in to_sides]
    far = len(to_each) + len(to_all)
    return pl.pallas_call(
        functools.partial(exchange_kernel, count, len(to_each), len(to_all), len(to_sides)),
        out_shape=[jax.ShapeDtypeStruct(s, x.dtype) for s, x in zip(shapes, ins)],
        in_specs=[ANY] * len(ins),
        out_specs=[ANY] * len(ins),
        scratch_shapes=[
            pltpu.SemaphoreType.DMA((max(far, 1), count)),
            pltpu.SemaphoreType.DMA((max(far, 1), count)),
            pltpu.SemaphoreType.DMA((max(far, 1),)),
            pltpu.SemaphoreType.DMA((2, max(len(to_sides), 1), 2)),
        ],
        compiler_params=pltpu.CompilerParams(collective_id=ident, has_side_effects=True),
        name="exchange",
    )(*ins)


def pick_kernel(block_of, a, b, out, sem):
    count = out.shape[0]

    def start(slot, carry):
        rows = pl.ds(pl.multiple_of(block_of[slot] * BLOCK, BLOCK), BLOCK)
        pltpu.make_async_copy(a.at[rows], out.at[slot, 0], sem).start()
        pltpu.make_async_copy(b.at[rows], out.at[slot, 1], sem).start()
        return carry

    lax.fori_loop(0, count, start, 0)
    pltpu.make_async_copy(out, out, sem).wait()


def pick(block_of, a, b):
    count = block_of.shape[0]
    return pl.pallas_call(
        pick_kernel,
        out_shape=jax.ShapeDtypeStruct((count, 2, BLOCK, a.shape[1]), a.dtype),
        in_specs=[SMEM] + [pl.BlockSpec(memory_space=pltpu.VMEM)] * 2,
        out_specs=ANY,
        scratch_shapes=[pltpu.SemaphoreType.DMA],
        cost_estimate=pl.CostEstimate(flops=0, bytes_accessed=16 << 20, transcendentals=0),
        name="pick",
    )(block_of, a, b)


def rows_kernel(
    order, off, group, q_in, k_in, v_in, g_in, edge_in, first_in, slot_in, first_out,
    out_ref, dq_ref, dk_ref, dv_ref, dk0_ref, dv0_ref, stat_ref,
    q, k, v, g, slot, kg, vg, near, nearp, link, linkp, top, total, acc, sem,
):
    heads = q.shape[1] // HEAD_DIM
    blocks = q.shape[0] // BLOCK
    frames = q.shape[0]
    own = group[0]
    last = group[1]
    copies = [
        pltpu.make_async_copy(q_in, q, sem.at[0]),
        pltpu.make_async_copy(g_in, g, sem.at[1]),
        pltpu.make_async_copy(k_in, k.at[pl.ds(BLOCK, frames)], sem.at[2]),
        pltpu.make_async_copy(v_in, v.at[pl.ds(BLOCK, frames)], sem.at[3]),
        pltpu.make_async_copy(edge_in.at[0, 0], k.at[pl.ds(0, BLOCK)], sem.at[4]),
        pltpu.make_async_copy(edge_in.at[0, 1], k.at[pl.ds(BLOCK + frames, BLOCK)], sem.at[5]),
        pltpu.make_async_copy(edge_in.at[1, 0], v.at[pl.ds(0, BLOCK)], sem.at[6]),
        pltpu.make_async_copy(edge_in.at[1, 1], v.at[pl.ds(BLOCK + frames, BLOCK)], sem.at[7]),
        pltpu.make_async_copy(first_in.at[1], kg, sem.at[8]),
        pltpu.make_async_copy(first_in.at[2], vg, sem.at[9]),
        pltpu.make_async_copy(slot_in, slot, sem.at[10]),
    ]
    for copy in copies:
        copy.start()
    dk_ref[...] = jnp.zeros_like(dk_ref)
    dv_ref[...] = jnp.zeros_like(dv_ref)
    dk0_ref[...] = jnp.zeros_like(dk0_ref)
    dv0_ref[...] = jnp.zeros_like(dv0_ref)
    for copy in copies:
        copy.wait()
    cols = [slice(h * HEAD_DIM, (h + 1) * HEAD_DIM) for h in range(heads)]
    band = 3 * BLOCK

    def row(i, carry):
        base = pl.multiple_of(i * BLOCK, BLOCK)
        rows = pl.ds(base, BLOCK)
        wide = pl.ds(base, band)
        row_id = own * blocks + i
        begin, end = off[i], off[i + 1]
        column_id = row_id - 1 + lax.broadcasted_iota(jnp.int32, (1, band), 1) // BLOCK
        bias = jnp.where((column_id > 0) & (column_id <= last), 0.0, NEG)
        keep = (row_id > 0).astype(F32)
        for h in range(heads):
            qh = q[rows, cols[h]]
            s = nt(qh, k[wide, cols[h]]) * SCALE + bias
            sg = nt(qh, kg[h]) * SCALE
            near[h, :, :band] = s
            near[h, :, band:] = sg
            top[h] = jnp.maximum(
                jnp.maximum(s[:, :BLOCK], s[:, BLOCK : 2 * BLOCK]),
                jnp.maximum(s[:, 2 * BLOCK :], sg),
            )

        def score(t, c):
            n = order[t]
            for h in range(heads):
                s = nt(q[rows, cols[h]], slot[n, 0, :, cols[h]]) * SCALE
                link[t - begin, h] = s
                top[h] = jnp.maximum(top[h], s)
            return c

        lax.fori_loop(begin, end, score, 0)
        tops = [jnp.max(top[h], axis=1, keepdims=True) for h in range(heads)]
        for h in range(heads):
            e = jnp.exp(near[h] - tops[h])
            total[h] = (e[:, :BLOCK] + e[:, BLOCK : 2 * BLOCK]) + (e[:, 2 * BLOCK : band] + e[:, band:])
            top[h] = jnp.broadcast_to(tops[h], (BLOCK, BLOCK))

        def expo(t, c):
            for h in range(heads):
                total[h] += jnp.exp(link[t - begin, h] - top[h])
            return c

        lax.fori_loop(begin, end, expo, 0)
        sums = [jnp.sum(total[h], axis=1, keepdims=True) for h in range(heads)]
        lses = [tops[h] + jnp.log(sums[h]) for h in range(heads)]
        for h in range(heads):
            top[h] = jnp.broadcast_to(lses[h], (BLOCK, BLOCK))
            w = (jnp.exp(near[h] - lses[h]) * keep).astype(BF16)
            nearp[h] = w
            acc[h] = nn(w[:, :band], v[wide, cols[h]]) + nn(w[:, band:], vg[h])

        def attend(t, c):
            n = order[t]
            for h in range(heads):
                w = jnp.exp(link[t - begin, h] - top[h]).astype(BF16)
                linkp[t - begin, h] = w
                acc[h] += nn(w, slot[n, 1, :, cols[h]])
            return c

        lax.fori_loop(begin, end, attend, 0)
        is_first = row_id == 0
        deltas = []
        for h in range(heads):
            o = jnp.where(is_first, first_out[h], acc[h]).astype(BF16)
            out_ref[rows, cols[h]] = o
            gh = g[rows, cols[h]]
            delta = jnp.sum(gh.astype(F32) * o.astype(F32), axis=1, keepdims=True)
            deltas.append(delta)
            total[h] = jnp.broadcast_to(delta, (BLOCK, BLOCK))
            qh = q[rows, cols[h]]
            w = nearp[h]
            gw = nt(gh, v[wide, cols[h]])
            gwg = nt(gh, vg[h])
            gs = (w[:, :band].astype(F32) * (gw - delta)).astype(BF16)
            gsg = (w[:, band:].astype(F32) * (gwg - delta)).astype(BF16)
            acc[h] = nn(gs, k[wide, cols[h]]) + nn(gsg, kg[h])
            dk_ref[wide, cols[h]] += tn(gs, qh)
            dv_ref[wide, cols[h]] += tn(w[:, :band], gh)
            dk0_ref[h] += tn(gsg, qh)
            dv0_ref[h] += tn(w[:, band:], gh)

        def backward(t, c):
            n = order[t]
            for h in range(heads):
                gw = nt(g[rows, cols[h]], slot[n, 1, :, cols[h]])
                gs = (linkp[t - begin, h].astype(F32) * (gw - total[h])).astype(BF16)
                acc[h] += nn(gs, slot[n, 0, :, cols[h]])
            return c

        lax.fori_loop(begin, end, backward, 0)
        lane = lax.broadcasted_iota(jnp.int32, (BLOCK, BLOCK), 1)
        packed = jnp.zeros((BLOCK, BLOCK), F32)
        for h in range(heads):
            dq_ref[rows, cols[h]] = (acc[h] * SCALE).astype(BF16)
            packed = jnp.where(lane == h, lses[h], packed)
            packed = jnp.where(lane == heads + h, deltas[h], packed)
        stat_ref[i] = packed.T[: 2 * heads]
        return carry

    lax.fori_loop(0, blocks, row, 0)


def own_rows(order, off, group, q, k, v, g, edge, first, slots, first_out):
    frames, width = q.shape
    heads, blocks, count = width // HEAD_DIM, frames // BLOCK, slots.shape[0]
    pad = frames + 2 * BLOCK
    tile = (heads, BLOCK, BLOCK)
    vmem = pl.BlockSpec(memory_space=pltpu.VMEM)
    return pl.pallas_call(
        rows_kernel,
        out_shape=[
            jax.ShapeDtypeStruct((frames, width), BF16),
            jax.ShapeDtypeStruct((frames, width), BF16),
            jax.ShapeDtypeStruct((pad, width), F32),
            jax.ShapeDtypeStruct((pad, width), F32),
            jax.ShapeDtypeStruct(tile, F32),
            jax.ShapeDtypeStruct(tile, F32),
            jax.ShapeDtypeStruct((blocks, 2 * heads, BLOCK), F32),
        ],
        in_specs=[SMEM] * 3 + [ANY] * 7 + [vmem],
        out_specs=[vmem] * 7,
        scratch_shapes=[
            pltpu.VMEM((frames, width), BF16),
            pltpu.VMEM((pad, width), BF16),
            pltpu.VMEM((pad, width), BF16),
            pltpu.VMEM((frames, width), BF16),
            pltpu.VMEM(slots.shape, BF16),
            pltpu.VMEM(tile, BF16),
            pltpu.VMEM(tile, BF16),
            pltpu.VMEM((heads, BLOCK, 4 * BLOCK), F32),
            pltpu.VMEM((heads, BLOCK, 4 * BLOCK), BF16),
            pltpu.VMEM((count,) + tile, F32),
            pltpu.VMEM((count,) + tile, BF16),
            pltpu.VMEM(tile, F32),
            pltpu.VMEM(tile, F32),
            pltpu.VMEM(tile, F32),
            pltpu.SemaphoreType.DMA((11,)),
        ],
        compiler_params=pltpu.CompilerParams(vmem_limit_bytes=56 << 20),
        cost_estimate=pl.CostEstimate(
            flops=20 << 30, bytes_accessed=24 << 20, transcendentals=8 << 20
        ),
        name="own_rows",
    )(order, off, group, q, k, v, g, edge, first, slots, first_out)


def columns_kernel(
    order, off, k_in, v_in, slot_in, stat_in, dk_in, dv_in, dk_ref, dv_ref,
    k, v, slot, stat, dk, dv, sem,
):
    heads = k.shape[1] // HEAD_DIM
    blocks = k.shape[0] // BLOCK
    pairs = ((k_in, k), (v_in, v), (slot_in, slot), (stat_in, stat), (dk_in, dk), (dv_in, dv))
    copies = [pltpu.make_async_copy(s, d, sem.at[n]) for n, (s, d) in enumerate(pairs)]
    for copy in copies:
        copy.start()
    for copy in copies:
        copy.wait()
    cols = [slice(h * HEAD_DIM, (h + 1) * HEAD_DIM) for h in range(heads)]

    def column(i, carry):
        rows = pl.ds(pl.multiple_of(i * BLOCK, BLOCK), BLOCK)

        def link(t, c):
            n = order[t]
            for h in range(heads):
                qs, gs = slot[n, 0, :, cols[h]], slot[n, 1, :, cols[h]]
                s = nt(k[rows, cols[h]], qs) * SCALE
                w = jnp.exp(s - stat[n, h : h + 1]).astype(BF16)
                gw = nt(v[rows, cols[h]], gs)
                d = (w.astype(F32) * (gw - stat[n, heads + h : heads + h + 1])).astype(BF16)
                dk[rows, cols[h]] += nn(d, qs)
                dv[rows, cols[h]] += nn(w, gs)
            return c

        lax.fori_loop(off[i], off[i + 1], link, 0)
        dk_ref[rows] = (dk[rows] * SCALE).astype(BF16)
        dv_ref[rows] = dv[rows].astype(BF16)
        return carry

    lax.fori_loop(0, blocks, column, 0)


def own_columns(order, off, k, v, slots, stats, dk, dv):
    frames, width = k.shape
    vmem = pl.BlockSpec(memory_space=pltpu.VMEM)
    return pl.pallas_call(
        columns_kernel,
        out_shape=[jax.ShapeDtypeStruct((frames, width), BF16)] * 2,
        in_specs=[SMEM] * 2 + [ANY] * 6,
        out_specs=[vmem] * 2,
        scratch_shapes=[
            pltpu.VMEM((frames, width), BF16),
            pltpu.VMEM((frames, width), BF16),
            pltpu.VMEM(slots.shape, BF16),
            pltpu.VMEM(stats.shape, F32),
            pltpu.VMEM((frames, width), F32),
            pltpu.VMEM((frames, width), F32),
            pltpu.SemaphoreType.DMA((6,)),
        ],
        compiler_params=pltpu.CompilerParams(vmem_limit_bytes=56 << 20),
        cost_estimate=pl.CostEstimate(
            flops=4 << 30, bytes_accessed=18 << 20, transcendentals=2 << 20
        ),
        name="own_columns",
    )(order, off, k, v, slots, stats, dk, dv)


def link_tables(rows, own, shards, per_dev):
    linked = rows.reshape(per_dev, shards, per_dev)
    block = jnp.arange(per_dev, dtype=jnp.int32)[:, None, None]
    peer = jnp.arange(shards, dtype=jnp.int32)[None, :, None]
    peer_block = jnp.arange(per_dev, dtype=jnp.int32)[None, None, :]
    own_id = own * per_dev + block
    peer_id = peer * per_dev + peer_block
    live = (
        (peer != own)
        & (linked > 0)
        & (own_id > 0)
        & (peer_id > 0)
        & (jnp.abs(own_id - peer_id) > 1)
    ).astype(jnp.int32)
    count = jnp.sum(live, axis=(0, 2))
    block_of = jnp.sum(live * block, axis=(0, 2))
    key = jnp.where(count > 0, block_of, per_dev)
    slot = jnp.arange(shards, dtype=jnp.int32)
    rank = jnp.sum(
        (
            (key[None, :] < key[:, None])
            | ((key[None, :] == key[:, None]) & (slot[None, :] < slot[:, None]))
        ).astype(jnp.int32),
        axis=1,
    )
    order = jnp.sum(slot[None, :] * (rank[None, :] == slot[:, None]).astype(jnp.int32), axis=1)
    off = jnp.sum(
        (key[None, :] < jnp.arange(per_dev + 1, dtype=jnp.int32)[:, None]).astype(jnp.int32), axis=1
    )
    return block_of, order, off


def body(query_in, key_in, value_in, out_grad, pattern):
    shards = lax.axis_size("seq")
    own = lax.axis_index("seq")
    total_blocks = pattern.shape[0]
    per_dev = total_blocks // shards
    is_first = own == 0
    rows = lax.dynamic_slice_in_dim(pattern, own * per_dev, per_dev, 0)
    block_of, order, off = link_tables(rows, own, shards, per_dev)
    group = jnp.stack((own, jnp.int32(total_blocks - 1)))

    query, key, value, grad = heads_in((query_in, key_in, value_in, out_grad), 1)
    frames, width = query.shape
    heads = width // HEAD_DIM
    edge, first = edges(query, key, value, grad, 2)
    first = first.reshape(4, heads, BLOCK, HEAD_DIM)
    q0, k0, v0, g0 = first[0], first[1], first[2], first[3]

    by_head = (frames, heads, HEAD_DIM)
    key_h, value_h = key.reshape(by_head), value.reshape(by_head)
    s0 = jnp.einsum("hqe,khe->hqk", q0, key_h, preferred_element_type=F32) * SCALE
    top0 = jnp.max(s0, axis=2)
    sum0 = jnp.sum(jnp.exp(s0 - top0[:, :, None]), axis=2)
    (parts,) = exchange(3, to_all=(jnp.concatenate((top0, sum0)),))
    tops = jnp.max(parts[:, :heads], axis=0)
    sums = jnp.sum(parts[:, heads:] * jnp.exp(parts[:, :heads] - tops[None]), axis=0)
    lse0 = tops + jnp.log(sums)
    w0 = jnp.exp(s0 - lse0[:, :, None]).astype(BF16)
    acc0 = jnp.einsum("hqk,khe->hqe", w0, value_h, preferred_element_type=F32)
    (acc_parts,) = exchange(4, to_each=(acc0.reshape(shards, 16, HEAD_DIM),))
    own_out = jnp.sum(acc_parts, axis=0).astype(BF16).astype(F32)
    (out_parts,) = exchange(5, to_all=(own_out,))
    out0 = out_parts.reshape(heads, BLOCK, HEAD_DIM)
    delta0 = jnp.sum(g0.astype(F32) * out0, axis=2)
    gw0 = jnp.einsum("hqe,khe->hqk", g0, value_h, preferred_element_type=F32)
    gs0 = (w0.astype(F32) * (gw0 - delta0[:, :, None])).astype(BF16)
    dq0 = jnp.einsum("hqk,khe->hqe", gs0, key_h, preferred_element_type=F32)
    dk_row0 = jnp.einsum("hqk,hqe->khe", gs0, q0, preferred_element_type=F32).reshape(frames, width)
    dv_row0 = jnp.einsum("hqk,hqe->khe", w0, g0, preferred_element_type=F32).reshape(frames, width)

    slot_kv = pick(block_of, key, value)
    slot_qg = pick(block_of, query, grad)
    slot_kv, out0 = lax.optimization_barrier((slot_kv, out0))
    recv_kv = lax.all_to_all(slot_kv, "seq", split_axis=0, concat_axis=0, tiled=True)
    slot_qg, recv_kv = lax.optimization_barrier((slot_qg, recv_kv))
    recv_qg = lax.all_to_all(slot_qg, "seq", split_axis=0, concat_axis=0, tiled=True)
    attended, dq, dk, dv, dk0, dv0, stats = own_rows(
        order, off, group, query, key, value, grad, edge, first, recv_kv, out0
    )
    slot_stats = jnp.take(stats, block_of, axis=0)
    unit = (shards, 16, HEAD_DIM)
    first_parts = jnp.stack((dq0.reshape(unit), dk0.reshape(unit), dv0.reshape(unit)), axis=1)
    low, high = slice(0, BLOCK), slice(BLOCK + frames, 2 * BLOCK + frames)
    sides = jnp.stack((jnp.stack((dk[high], dv[high])), jnp.stack((dk[low], dv[low]))))
    stats_in, first_sums, from_sides = exchange(
        6, to_each=(slot_stats, first_parts), to_sides=(sides,)
    )
    (totals,) = exchange(7, to_all=(jnp.sum(first_sums, axis=0),))
    totals = jnp.transpose(totals.reshape(heads, 8, 3, 16, HEAD_DIM), (2, 1, 3, 0, 4))
    totals = totals.reshape(3, BLOCK, width)
    totals = jnp.where(is_first, totals, 0.0)
    from_left = jnp.where(is_first, 0.0, from_sides[0])
    from_right = jnp.where(own == shards - 1, 0.0, from_sides[1])
    dk = dk[BLOCK : BLOCK + frames] + dk_row0
    dk = dk.at[:BLOCK].add(from_left[0] + totals[1]).at[frames - BLOCK :].add(from_right[0])
    dv = dv[BLOCK : BLOCK + frames] + dv_row0
    dv = dv.at[:BLOCK].add(from_left[1] + totals[2]).at[frames - BLOCK :].add(from_right[1])
    dq = dq.at[:BLOCK].set(jnp.where(is_first, (totals[0] * SCALE).astype(BF16), dq[:BLOCK]))
    attended_out, dq_out = heads_out((attended, dq), 8)
    dk, dv, attended_out, dq_out, recv_qg = lax.optimization_barrier(
        (dk, dv, attended_out, dq_out, recv_qg)
    )
    dk, dv = own_columns(order, off, key, value, recv_qg, stats_in, dk, dv)
    dk_out, dv_out = heads_out((dk, dv), 9)
    return attended_out, dq_out, dk_out, dv_out


def solution(mesh):
    split = P(("seq", "head"), None)
    return jax.shard_map(
        body,
        mesh=mesh,
        in_specs=(split, split, split, split, P()),
        out_specs=(split, split, split, split),
        check_vma=False,
    )
```

```python
import functools

import jax
import jax.numpy as jnp
from jax import lax
from jax.experimental import pallas as pl
from jax.experimental.pallas import tpu as pltpu
from jax.sharding import PartitionSpec as P

D = 128
B = 128
HEADS = 4
BLOCKS = 8
SEQ = 32
YS = 4
SCALE = D ** (-0.5)
NEG = -1e30
MESH = pl.DeviceIdType.MESH
F32, BF16 = jnp.float32, jnp.bfloat16
KV, QG = 0, 1
GROUPS = ((KV, 0), (KV, 1), (QG, 0), (KV, 2), (QG, 1), (KV, 3), (QG, 2), (QG, 3))
ARRIVALS = ((KV, 0), (KV, 1), (QG, 0), (KV, 2), (KV, 3), (QG, 1), (QG, 2), (QG, 3))
PER_GROUP = 4
BATCHES = ((1, 8), (8, 16), (16, 24), (24, 32))
RING = 4
EARLY = 3
AHEAD = 4


def nt(a, b):
    return lax.dot_general(a, b, (((1,), (1,)), ((), ())), preferred_element_type=F32)


def tn(a, b):
    return lax.dot_general(a, b, (((0,), (0,)), ((), ())), preferred_element_type=F32)


def nn(a, b):
    return jnp.dot(a, b, preferred_element_type=F32)


def loop(count, step, init, by=4):
    def some(n, carry):
        for m in range(by):
            carry = step(n * by + m, carry)
        return carry

    return lax.fori_loop(0, count // by, some, init)


def take_all(ref, sem):
    pltpu.make_async_copy(ref, ref, sem).wait()


def kernel(
    block_of, order, key, same, tail, has, live,
    k_in, v_in, q_in, g_in, o_out, dq_out, dk_out, dv_out,
    kv, qg, edge, stage, got, stat_out, stat_got, dgrad, side, staged,
    kpad, ns, npr, ls, lp, run_a, run_b, topb, lseb, delb, oacc, stat,
    fb, first, p0, ml_out, ml_got, acc_out, acc_got, o_own, o0, dq0, dk0, dv0,
    rs_out, rs_got, t_own, t_got,
    y_send, y_recv, y_local, fb_sem, sc_sem, ag_sem, bulk_send, bulk_recv, halo_sem, side_sem,
    ml_sem, acc_sem, o_sem, stat_sem, rs_sem, t_sem, out_sem,
):
    me, ym = lax.axis_index("seq"), lax.axis_index("head")
    mz, mx, mc = me // 8, lax.rem(me // 2, 4), lax.rem(me, 2)
    right, left = lax.rem(me + 1, SEQ), lax.rem(me + SEQ - 1, SEQ)
    ins = ((k_in, v_in), (q_in, g_in))
    own = (kv, qg)
    outs = (o_out, dq_out, dk_out, dv_out)
    is_root = me == 0

    def to_seq(src, dst, send, recv, peer):
        return pltpu.make_async_remote_copy(
            src_ref=src, dst_ref=dst, send_sem=send, recv_sem=recv,
            device_id={"seq": peer}, device_id_type=MESH,
        )

    def to_head(src, dst, send, recv, peer):
        return pltpu.make_async_remote_copy(
            src_ref=src, dst_ref=dst, send_sem=send, recv_sem=recv,
            device_id={"head": peer}, device_id_type=MESH,
        )

    def to_all(copy_to):
        def start(step, c):
            copy_to(lax.rem(me + step, SEQ)).start()
            return c

        lax.fori_loop(1, SEQ, start, 0)

    sem = pltpu.get_barrier_semaphore()

    def greet(step, c):
        pl.semaphore_signal(
            sem, inc=1, device_id={"seq": lax.rem(me + step, SEQ)}, device_id_type=MESH
        )
        return c

    lax.fori_loop(1, SEQ, greet, 0)
    for step in range(1, YS):
        pl.semaphore_signal(
            sem, inc=1, device_id={"head": lax.rem(ym + step, YS)}, device_id_type=MESH
        )
    pl.semaphore_wait(sem, SEQ - 1 + YS - 1)

    def columns(y, h):
        return pl.ds(pl.multiple_of((y * HEADS + h) * D, D), D)

    @pl.when(is_root & (ym == 0))
    def _():
        for p in range(2):
            for a in range(2):

                def give(n, c, p=p, a=a):
                    to_head(
                        ins[p][a].at[0, :, pl.ds(pl.multiple_of(n * D, D), D)],
                        fb.at[2 * p + a, lax.rem(n, HEADS)],
                        fb_sem.at[0], fb_sem.at[1], n // HEADS,
                    ).start()
                    return c

                lax.fori_loop(HEADS, YS * HEADS, give, 0)

                def hold(h, c, p=p, a=a):
                    pltpu.make_async_copy(
                        ins[p][a].at[0, :, pl.ds(pl.multiple_of(h * D, D), D)],
                        fb.at[2 * p + a, h],
                        fb_sem.at[2],
                    ).start()
                    return c

                lax.fori_loop(0, HEADS, hold, 0)

    def enter(p, h):
        for a in range(2):

            def give(step, c, a=a):
                peer = lax.rem(ym + step, YS)
                to_head(
                    ins[p][a].at[:, :, columns(peer, h)],
                    own[p][h].at[a, pl.ds(2 * ym, 2)],
                    y_send.at[p, h], y_recv.at[p, h], peer,
                ).start()
                return c

            lax.fori_loop(1, YS, give, 0)
            pltpu.make_async_copy(
                ins[p][a].at[:, :, columns(ym, h)],
                own[p][h].at[a, pl.ds(2 * ym, 2)],
                y_local.at[p, h],
            ).start()

    entering = list(ARRIVALS)

    def enter_next():
        if entering:
            enter(*entering.pop(0))

    for _ in range(EARLY):
        enter_next()
    for h in range(HEADS):
        for p in range(2):
            for n in range(BLOCKS + 2):
                dgrad[h][p, n] = jnp.zeros((B, D), F32)
    dk0[...] = jnp.zeros_like(dk0)
    dv0[...] = jnp.zeros_like(dv0)

    arrived = set()

    def arrive(p, h):
        if (p, h) in arrived:
            return
        arrived.add((p, h))
        enter_next()
        take_all(own[p][h].at[:, pl.ds(0, 6)], y_recv.at[p, h])
        take_all(own[p][h].at[:, pl.ds(0, 2)], y_local.at[p, h])
        if p == KV:
            to_seq(
                kv[h].at[:, BLOCKS - 1], edge[h].at[0], halo_sem.at[0, h], halo_sem.at[1, h], right
            ).start()
            to_seq(
                kv[h].at[:, 0], edge[h].at[1], halo_sem.at[2, h], halo_sem.at[3, h], left
            ).start()

    state = {"next": 0, "picked": 0}

    def sent(batch):
        begin, end = BATCHES[batch % PER_GROUP]
        buffer = stage[(batch // PER_GROUP) % RING]
        take_all(buffer.at[pl.ds(0, end - begin)], bulk_send.at[batch])

    def choose(n):
        p, h = GROUPS[n]
        arrive(p, h)
        buffer = stage[n % RING]

        def one(s, c):
            buffer[s, 0] = own[p][h][0, block_of[s]]
            buffer[s, 1] = own[p][h][1, block_of[s]]
            return c

        lax.fori_loop(0, SEQ, one, 0)

    def pump(upto=None):
        batch = state["next"]
        if batch >= PER_GROUP * len(GROUPS):
            return
        if upto is not None:
            while state["next"] < min(upto, PER_GROUP * len(GROUPS)):
                pump()
            return
        state["next"] += 1
        if batch >= AHEAD:
            sent(batch - AHEAD)
        n = batch // PER_GROUP
        if batch % PER_GROUP == 0:
            choose(n)
        p, h = GROUPS[n]

        def start(step, c):
            z = lax.rem(step, 4)
            x = lax.rem(step // 4 + z, 4)
            peer = lax.rem(mz + z, 4) * 8 + lax.rem(mx + x, 4) * 2 + lax.rem(mc + step // 16, 2)
            to_seq(
                stage[n % RING].at[peer], got[p][h].at[me],
                bulk_send.at[batch], bulk_recv.at[p, h], peer,
            ).start()
            return c

        lax.fori_loop(*BATCHES[batch % PER_GROUP], start, 0)

    posted = {}

    def post(name):
        posted[name] = state["next"]

    def due(name):
        pump(posted[name] + AHEAD)

    landed = set()

    def linked(p, h):
        if (p, h) in landed:
            return
        landed.add((p, h))
        n = GROUPS.index((p, h))
        pump(PER_GROUP * (n + 1) + AHEAD - 1)
        take_all(got[p][h].at[pl.ds(0, SEQ - 1)], bulk_recv.at[p, h])

    def piece(ref, unit):
        rows = pl.ds(pl.multiple_of(lax.rem(unit, 8) * 16, 16), 16)
        return ref.at[:, unit // 8, rows]

    @pl.when(is_root)
    def _():
        @pl.when(ym == 0)
        def _():
            take_all(fb, fb_sem.at[2])

        @pl.when(ym > 0)
        def _():
            take_all(fb, fb_sem.at[1])

        to_all(
            lambda peer: to_seq(piece(fb, peer), piece(first, peer), sc_sem.at[0], sc_sem.at[1], peer)
        )
        first[:, 0, pl.ds(0, 16)] = fb[:, 0, pl.ds(0, 16)]

    @pl.when(me > 0)
    def _():
        take_all(piece(first, me), sc_sem.at[1])

    to_all(lambda peer: to_seq(piece(first, me), piece(first, me), ag_sem.at[0], ag_sem.at[1], peer))
    arrive(KV, 0)
    pump(PER_GROUP)

    @pl.when(is_root & (ym == 0))
    def _():
        take_all(stage[1].at[pl.ds(0, 24)], fb_sem.at[0])

    arrive(KV, 1)
    pump()
    arrive(QG, 0)
    arrive(KV, 2)
    pump()
    arrive(KV, 3)
    pieces = lp.at[pl.ds(0, SEQ - 1), pl.ds(0, B // 2)]
    take_all(pieces, ag_sem.at[1])

    lanes = lax.broadcasted_iota(jnp.int32, (B, B), 1)

    def scores0(h, n):
        return nt(first[2, h], kv[h][0, n]) * SCALE

    packed = jnp.zeros((B, B), F32)
    for h in range(HEADS):
        tops = loop(BLOCKS, lambda n, c, h=h: jnp.maximum(c, scores0(h, n)), jnp.full((B, B), NEG, F32))
        m0 = jnp.max(tops, axis=1, keepdims=True)
        l0 = loop(BLOCKS, lambda n, c, h=h, m0=m0: c + jnp.exp(scores0(h, n) - m0), jnp.zeros((B, B), F32))
        packed = jnp.where(lanes == h, m0, packed)
        packed = jnp.where(lanes == HEADS + h, jnp.sum(l0, axis=1, keepdims=True), packed)
    ml_out[...] = packed.T[: 2 * HEADS]
    to_all(lambda peer: to_seq(ml_out, ml_got.at[me], ml_sem.at[0], ml_sem.at[1], peer))
    ml_got[me] = ml_out[...]
    post("ml")

    def rows_one(h):
        linked(KV, h)
        take_all(edge[h].at[0], halo_sem.at[1, h])
        take_all(edge[h].at[1], halo_sem.at[3, h])
        slot = got[KV][h]
        arrive(QG, h)
        for a in range(2):
            kpad[a, 0] = edge[h][0, a]
            kpad[a, pl.ds(1, BLOCKS)] = kv[h][a]
            kpad[a, BLOCKS + 1] = edge[h][1, a]

        def score(t, c):
            s = nt(qg[h][0, key[t]], slot[order[t], 0]) * SCALE
            s = s + jnp.where(t < live[0], 0.0, NEG)
            ls[t] = s
            run_a[t + 1] = jnp.maximum(s, run_a[t] + jnp.where(same[t] > 0, 0.0, NEG))
            return c

        run_a[0] = jnp.zeros((B, B), F32)
        loop(SEQ, score, 0)
        pump()

        def near_score(i, c):
            q = qg[h][0, i]
            band = kpad[0, pl.ds(i, 3)].reshape(3 * B, D)
            ids = me * BLOCKS + i - 1 + lax.broadcasted_iota(jnp.int32, (1, 3 * B), 1) // B
            s = nt(q, band) * SCALE + jnp.where((ids > 0) & (ids < SEQ * BLOCKS), 0.0, NEG)
            sg = nt(q, first[0, h]) * SCALE
            ns[i, :, pl.ds(0, 3 * B)] = s
            ns[i, :, pl.ds(3 * B, B)] = sg
            top = jnp.maximum(
                jnp.maximum(s[:, :B], s[:, B : 2 * B]), jnp.maximum(s[:, 2 * B :], sg)
            )
            top = jnp.maximum(top, jnp.where(has[i] > 0, run_a[tail[i]], NEG))
            topb[i] = jnp.broadcast_to(jnp.max(top, axis=1, keepdims=True), (B, B))
            return c

        loop(BLOCKS, near_score, 0, by=2)

        def expo(t, c):
            e = jnp.exp(ls[t] - topb[key[t]])
            run_a[t + 1] = e + run_a[t] * same[t].astype(F32)
            return c

        loop(SEQ, expo, 0)
        pump()

        def near_weights(i, c):
            m = topb[i][:, :1]
            e = jnp.exp(ns[i] - m)
            e = (e[:, :B] + e[:, B : 2 * B]) + (e[:, 2 * B : 3 * B] + e[:, 3 * B :])
            e = e + jnp.where(has[i] > 0, run_a[tail[i]], 0.0)
            lse = m + jnp.log(jnp.sum(e, axis=1, keepdims=True))
            lseb[i] = jnp.broadcast_to(lse, (B, B))
            keep = jnp.where(me * BLOCKS + i > 0, 1.0, 0.0)
            w = (jnp.exp(ns[i] - lse) * keep).astype(BF16)
            npr[i] = w
            oacc[i] = nn(w[:, : 3 * B], kpad[1, pl.ds(i, 3)].reshape(3 * B, D)) + nn(
                w[:, 3 * B :], first[1, h]
            )
            return c

        loop(BLOCKS, near_weights, 0, by=2)

        def attend(t, c):
            w = jnp.exp(ls[t] - lseb[key[t]]).astype(BF16)
            lp[t] = w
            run_a[t + 1] = nn(w, slot[order[t], 1]) + run_a[t] * same[t].astype(F32)
            return c

        loop(SEQ, attend, 0)
        pump()

        def near_back(i, c):
            o = (oacc[i] + jnp.where(has[i] > 0, run_a[tail[i]], 0.0)).astype(BF16)
            staged[0][h][i] = o
            g, q = qg[h][1, i], qg[h][0, i]
            delta = jnp.sum(g.astype(F32) * o.astype(F32), axis=1, keepdims=True)
            delb[i] = jnp.broadcast_to(delta, (B, B))
            both = jnp.where(lanes == 0, lseb[i], delb[i])
            stat[i] = both.T[:8]
            w = npr[i]
            gw = nt(g, kpad[1, pl.ds(i, 3)].reshape(3 * B, D))
            gwg = nt(g, first[1, h])
            gs = (w[:, : 3 * B].astype(F32) * (gw - delta)).astype(BF16)
            gsg = (w[:, 3 * B :].astype(F32) * (gwg - delta)).astype(BF16)
            oacc[i] = nn(gs, kpad[0, pl.ds(i, 3)].reshape(3 * B, D)) + nn(gsg, first[0, h])
            dgrad[h][0, pl.ds(i, 3)] += tn(gs, q).reshape(3, B, D)
            dgrad[h][1, pl.ds(i, 3)] += tn(w[:, : 3 * B], g).reshape(3, B, D)
            dk0[h] += tn(gsg, q)
            dv0[h] += tn(w[:, 3 * B :], g)
            return c

        loop(BLOCKS, near_back, 0, by=2)

        def stat_of(s, c):
            stat_out[h][s] = stat[block_of[s]]
            return c

        lax.fori_loop(0, SEQ, stat_of, 0)
        to_all(
            lambda peer: to_seq(
                stat_out[h].at[peer], stat_got[h].at[me], stat_sem.at[0, h], stat_sem.at[1, h], peer
            )
        )
        stat_got[h][me] = stat_out[h][me]
        post(("stat", h))
        to_seq(
            dgrad[h].at[:, BLOCKS + 1], side[h].at[0], side_sem.at[0, h], side_sem.at[1, h], right
        ).start()
        to_seq(dgrad[h].at[:, 0], side[h].at[1], side_sem.at[2, h], side_sem.at[3, h], left).start()
        pump()

        def back(t, c):
            gw = nt(qg[h][1, key[t]], slot[order[t], 1])
            gs = (lp[t].astype(F32) * (gw - delb[key[t]])).astype(BF16)
            run_a[t + 1] = nn(gs, slot[order[t], 0]) + run_a[t] * same[t].astype(F32)
            return c

        loop(SEQ, back, 0)

        def query_grad(i, c):
            dq = oacc[i] + jnp.where(has[i] > 0, run_a[tail[i]], 0.0)
            staged[1][h][i] = (dq * SCALE).astype(BF16)
            return c

        loop(BLOCKS, query_grad, 0)

    def leave(a, h, step, block):
        peer = lax.rem(ym + step, YS)
        return to_head(
            staged[a][h].at[pl.ds(2 * peer + block, 1)],
            outs[a].at[pl.ds(block, 1), :, columns(ym, h)],
            out_sem.at[0, a], out_sem.at[1, a], peer,
        )

    def remain(a, h, block):
        return pltpu.make_async_copy(
            staged[a][h].at[pl.ds(2 * ym + block, 1)],
            outs[a].at[pl.ds(block, 1), :, columns(ym, h)],
            out_sem.at[2, a],
        )

    def depart(a, h):
        remain(a, h, 1).start()

        def ahead(step, c):
            leave(a, h, step, 1).start()
            return c

        lax.fori_loop(1, YS, ahead, 0)

        @pl.when(jnp.logical_not(is_root & (ym == 0)) | (a == 0))
        def _():
            remain(a, h, 0).start()

        def rest(step, c):
            @pl.when(jnp.logical_not(is_root & (lax.rem(ym + step, YS) == 0)) | (a == 0))
            def _():
                leave(a, h, step, 0).start()

            return c

        lax.fori_loop(1, YS, rest, 0)

    def columns_one(h):
        linked(QG, h)
        due(("stat", h))
        take_all(stat_got[h].at[pl.ds(0, SEQ - 1)], stat_sem.at[1, h])
        slot, stats = got[QG][h], stat_got[h]

        def link(t, c):
            n, b = order[t], key[t]
            q, g = slot[n, 0], slot[n, 1]
            st = stats[n]
            s = nt(kv[h][0, b], q) * SCALE
            w = jnp.exp(s - st[0:1]).astype(BF16)
            gw = nt(kv[h][1, b], g)
            d = (w.astype(F32) * (gw - st[1:2])).astype(BF16)
            f = same[t].astype(F32)
            run_a[t + 1] = nn(d, q) + run_a[t] * f
            run_b[t + 1] = nn(w, g) + run_b[t] * f
            return c

        run_a[0] = jnp.zeros((B, D), F32)
        run_b[0] = jnp.zeros((B, D), F32)
        loop(SEQ, link, 0)
        pump()
        take_all(side[h].at[0], side_sem.at[1, h])
        take_all(side[h].at[1], side_sem.at[3, h])
        not_first = jnp.where(me > 0, 1.0, 0.0)
        not_last = jnp.where(me < SEQ - 1, 1.0, 0.0)

        def final(i, c):
            at_low = jnp.where(i == 0, not_first, 0.0)
            at_high = jnp.where(i == BLOCKS - 1, not_last, 0.0)
            for a, run in enumerate((run_a, run_b)):
                d = dgrad[h][a, i + 1] + jnp.where(has[i] > 0, run[tail[i]], 0.0)
                d = d + side[h][0, a] * at_low + side[h][1, a] * at_high
                dgrad[h][a, i + 1] = d
                staged[2 + a][h][i] = (d * (SCALE if a == 0 else 1.0)).astype(BF16)
            return c

        loop(BLOCKS, final, 0, by=2)
        depart(2, h)
        depart(3, h)

    rows_one(0)

    due("ml")
    take_all(ml_got.at[pl.ds(0, SEQ - 1)], ml_sem.at[1])
    parts = ml_got[...]
    tops = jnp.max(parts[:, :HEADS], axis=0)
    sums = jnp.sum(parts[:, HEADS:] * jnp.exp(parts[:, :HEADS] - tops[None]), axis=0)
    lse_rows = jnp.concatenate((tops + jnp.log(sums), jnp.zeros((B - HEADS, B), F32)))
    lse_cols = lse_rows.T
    for h in range(HEADS):
        lse = lse_cols[:, h : h + 1]

        def weigh(n, c, h=h, lse=lse):
            w = jnp.exp(scores0(h, n) - lse).astype(BF16)
            p0[h, n] = w
            return c + nn(w, kv[h][1, n])

        a0 = loop(BLOCKS, weigh, jnp.zeros((B, D), F32))
        acc_out[pl.ds(h * 8, 8)] = a0.reshape(8, 16, D)
    to_all(
        lambda peer: to_seq(acc_out.at[peer], acc_got.at[me], acc_sem.at[0], acc_sem.at[1], peer)
    )
    acc_got[me] = acc_out[me]
    post("acc")

    rows_one(1)

    due("acc")
    take_all(acc_got.at[pl.ds(0, SEQ - 1)], acc_sem.at[1])
    o_own[...] = jnp.sum(acc_got[...], axis=0).astype(BF16).astype(F32)
    to_all(lambda peer: to_seq(o_own, o0.at[me], o_sem.at[0], o_sem.at[1], peer))
    o0[me] = o_own[...]
    post("o")
    linked(QG, 0)
    due("o")
    take_all(o0.at[pl.ds(0, SEQ - 1)], o_sem.at[1])

    for h in range(HEADS):
        g, q = first[3, h], first[2, h]
        o = o0[pl.ds(h * 8, 8)].reshape(B, D)
        delta = jnp.sum(g.astype(F32) * o, axis=1, keepdims=True)

        def back0(n, c, h=h, g=g, q=q, delta=delta):
            w = p0[h, n]
            gs = (w.astype(F32) * (nt(g, kv[h][1, n]) - delta)).astype(BF16)
            dgrad[h][0, n + 1] += tn(gs, q)
            dgrad[h][1, n + 1] += tn(w, g)
            return c + nn(gs, kv[h][0, n])

        dq0[h] = loop(BLOCKS, back0, jnp.zeros((B, D), F32), by=2)

    def departs(h):
        @pl.when(is_root)
        def _():
            staged[0][h][0] = o0[pl.ds(h * 8, 8)].reshape(B, D).astype(BF16)

        depart(0, h)
        depart(1, h)

    departs(0)
    departs(1)
    pump()

    columns_one(0)
    rows_one(2)
    departs(2)
    columns_one(1)
    rows_one(3)
    departs(3)

    for h in range(HEADS):
        for n, ref in enumerate((dq0, dk0, dv0)):
            rs_out[pl.ds(h * 8, 8), n] = ref[h].reshape(8, 16, D)
    to_all(lambda peer: to_seq(rs_out.at[peer], rs_got.at[me], rs_sem.at[0], rs_sem.at[1], peer))
    rs_got[me] = rs_out[me]
    columns_one(2)
    pump(PER_GROUP * len(GROUPS))
    take_all(rs_got.at[pl.ds(0, SEQ - 1)], rs_sem.at[1])
    t_own[...] = jnp.sum(rs_got[...], axis=0)

    @pl.when(me > 0)
    def _():
        to_seq(t_own, t_got.at[me], t_sem.at[0], t_sem.at[1], 0).start()

    columns_one(3)

    @pl.when(is_root)
    def _():
        t_got[0] = t_own[...]
        take_all(t_got.at[pl.ds(0, SEQ - 1)], t_sem.at[1])
        for h in range(HEADS):
            dq, dk, dv = (t_got[pl.ds(h * 8, 8), n].reshape(B, D) for n in range(3))
            staged[1][h][0] = (dq * SCALE).astype(BF16)
            staged[2][h][0] = ((dgrad[h][0, 1] + dk) * SCALE).astype(BF16)
            staged[3][h][0] = (dgrad[h][1, 1] + dv).astype(BF16)
        for a in range(1, 4):
            for h in range(HEADS):
                @pl.when(ym == 0)
                def _(a=a, h=h):
                    remain(a, h, 0).start()

                @pl.when(ym > 0)
                def _(a=a, h=h):
                    leave(a, h, YS - ym, 0).start()

    for p, h in ARRIVALS:
        take_all(own[p][h].at[:, pl.ds(0, 6)], y_send.at[p, h])
    for batch in range(PER_GROUP * len(GROUPS) - AHEAD, PER_GROUP * len(GROUPS)):
        sent(batch)
    for h in range(HEADS):
        take_all(edge[h].at[0], halo_sem.at[0, h])
        take_all(edge[h].at[1], halo_sem.at[2, h])
        take_all(side[h].at[0], side_sem.at[0, h])
        take_all(side[h].at[1], side_sem.at[2, h])
        take_all(stat_got[h].at[pl.ds(0, SEQ - 1)], stat_sem.at[0, h])
    take_all(pieces, ag_sem.at[0])

    @pl.when(is_root)
    def _():
        take_all(pieces, sc_sem.at[0])

    @pl.when(me > 0)
    def _():
        take_all(t_own, t_sem.at[0])

    take_all(ml_got.at[pl.ds(0, SEQ - 1)], ml_sem.at[0])
    take_all(acc_got.at[pl.ds(0, SEQ - 1)], acc_sem.at[0])
    take_all(o0.at[pl.ds(0, SEQ - 1)], o_sem.at[0])
    take_all(rs_got.at[pl.ds(0, SEQ - 1)], rs_sem.at[0])
    for a in range(4):
        most, rest = pl.ds(0, 3 * HEADS * D), pl.ds(0, HEADS * D)
        take_all(outs[a].at[:, :, most], out_sem.at[0, a])
        take_all(outs[a].at[:, :, most], out_sem.at[1, a])
        take_all(outs[a].at[:, :, rest], out_sem.at[2, a])


def link_tables(rows, own):
    linked = rows.reshape(BLOCKS, SEQ, BLOCKS)
    block = jnp.arange(BLOCKS, dtype=jnp.int32)[:, None, None]
    peer = jnp.arange(SEQ, dtype=jnp.int32)[None, :, None]
    peer_block = jnp.arange(BLOCKS, dtype=jnp.int32)[None, None, :]
    own_id = own * BLOCKS + block
    peer_id = peer * BLOCKS + peer_block
    live = (
        (peer != own)
        & (linked > 0)
        & (own_id > 0)
        & (peer_id > 0)
        & (jnp.abs(own_id - peer_id) > 1)
    ).astype(jnp.int32)
    block_of = jnp.sum(live * block, axis=(0, 2))
    raw = jnp.where(jnp.sum(live, axis=(0, 2)) > 0, block_of, BLOCKS)
    slot = jnp.arange(SEQ, dtype=jnp.int32)
    before = (raw[None, :] < raw[:, None]) | (
        (raw[None, :] == raw[:, None]) & (slot[None, :] < slot[:, None])
    )
    rank = jnp.sum(before.astype(jnp.int32), axis=1)
    place = (rank[None, :] == slot[:, None]).astype(jnp.int32)
    order = jnp.sum(slot[None, :] * place, axis=1)
    key = jnp.sum(raw[None, :] * place, axis=1)
    same = jnp.concatenate((jnp.zeros((1,), jnp.int32), (key[1:] == key[:-1]).astype(jnp.int32)))
    bounds = jnp.arange(BLOCKS + 1, dtype=jnp.int32)
    off = jnp.sum((raw[None, :] < bounds[:, None]).astype(jnp.int32), axis=1)
    has = (off[1:] > off[:-1]).astype(jnp.int32)
    tail = off[1:]
    return block_of, order, jnp.minimum(key, BLOCKS - 1), same, tail, has, off[BLOCKS:]


def body(query_in, key_in, value_in, out_grad, pattern):
    own = lax.axis_index("seq")
    rows = lax.dynamic_slice_in_dim(pattern, own * BLOCKS, BLOCKS, 0)
    tables = link_tables(rows, own)
    shape = (2, B, YS * HEADS * D)
    arrays = [x.reshape(shape) for x in (key_in, value_in, query_in, out_grad)]
    dma = pltpu.SemaphoreType.DMA
    vm = pltpu.VMEM

    def each(shape, dtype):
        return [vm(shape, dtype) for _ in range(HEADS)]

    tile = (B, D)
    scratch = [
        each((2, BLOCKS) + tile, BF16),
        each((2, BLOCKS) + tile, BF16),
        each((2, 2) + tile, BF16),
        [vm((SEQ, 2) + tile, BF16) for _ in range(RING)],
        [each((SEQ, 2) + tile, BF16), each((SEQ, 2) + tile, BF16)],
        each((SEQ, 8, B), F32),
        each((SEQ, 8, B), F32),
        each((2, BLOCKS + 2) + tile, F32),
        each((2, 2) + tile, F32),
        [each((BLOCKS,) + tile, BF16) for _ in range(4)],
        vm((2, BLOCKS + 2) + tile, BF16),
        vm((BLOCKS, B, 4 * B), F32),
        vm((BLOCKS, B, 4 * B), BF16),
        vm((SEQ, B, B), F32),
        vm((SEQ, B, B), BF16),
        vm((SEQ + 1, B, D), F32),
        vm((SEQ + 1, B, D), F32),
        vm((BLOCKS, B, B), F32),
        vm((BLOCKS, B, B), F32),
        vm((BLOCKS, B, B), F32),
        vm((BLOCKS, B, D), F32),
        vm((BLOCKS, 8, B), F32),
        vm((4, HEADS) + tile, BF16),
        vm((4, HEADS) + tile, BF16),
        vm((HEADS, BLOCKS, B, B), BF16),
        vm((8, B), F32),
        vm((SEQ, 8, B), F32),
        vm((SEQ, 16, D), F32),
        vm((SEQ, 16, D), F32),
        vm((16, D), F32),
        vm((SEQ, 16, D), F32),
        vm((HEADS,) + tile, F32),
        vm((HEADS,) + tile, F32),
        vm((HEADS,) + tile, F32),
        vm((SEQ, 3, 16, D), F32),
        vm((SEQ, 3, 16, D), F32),
        vm((3, 16, D), F32),
        vm((SEQ, 3, 16, D), F32),
        dma((2, HEADS)),
        dma((2, HEADS)),
        dma((2, HEADS)),
        dma((3,)),
        dma((2,)),
        dma((2,)),
        dma((PER_GROUP * len(GROUPS),)),
        dma((2, HEADS)),
        dma((4, HEADS)),
        dma((4, HEADS)),
        dma((2,)),
        dma((2,)),
        dma((2,)),
        dma((2, HEADS)),
        dma((2,)),
        dma((2,)),
        dma((3, 4)),
    ]
    any_space = pl.BlockSpec(memory_space=pl.ANY)
    results = pl.pallas_call(
        kernel,
        out_shape=[jax.ShapeDtypeStruct(shape, BF16)] * 4,
        in_specs=[pl.BlockSpec(memory_space=pltpu.SMEM)] * len(tables) + [any_space] * 4,
        out_specs=[any_space] * 4,
        scratch_shapes=scratch,
        compiler_params=pltpu.CompilerParams(
            collective_id=0, has_side_effects=True, vmem_limit_bytes=62 << 20
        ),
        name="sparse_attention",
    )(*tables, *arrays)
    return tuple(x.reshape(query_in.shape) for x in results)


def solution(mesh):
    split = P(("seq", "head"), None)
    return jax.shard_map(
        body,
        mesh=mesh,
        in_specs=(split, split, split, split, P()),
        out_specs=(split, split, split, split),
        check_vma=False,
    )
```
